32 devices in a mesh: slab: 2 (over x), phase: 16 (over z, y, core).
Axes of the slice: x: 2, y: 2, z: 4, core: 2. Of those that a mesh axis runs over, the one named last changes fastest.
Arguments:
- estimate: float32 [32, 256, 512], P(('slab', 'phase')), parts along dimension 0, may hold values from -6 to 6
- kdata: float32 [32, 32, 256, 512], P('slab', 'phase'), parts along dimension 0, may hold values from -4 to 4
- maps: float32 [64, 256, 512], P(('slab', 'phase')), parts along dimension 0, may hold values from -1 to 1
- mask: int32 [32, 256], P('slab'), parts along dimension 0, may hold values 0 or 1
- w_first: bfloat16 [16, 2, 3, 3, 3], replicated, may hold values from -0.875 to 0.875
- w_middle: bfloat16 [16, 16, 3, 3, 3], replicated, may hold values from -0.3125 to 0.3125
- w_last: bfloat16 [2, 16, 3, 3, 3], replicated, may hold values from -0.3125 to 0.3125
Outputs:
- updated: float32 [32, 256, 512], P(('slab', 'phase')), parts along dimension 0
The draws below stay inside these ranges and needn't reach their ends.
There are 2 independent parts, one for each index of `slab`. The reference program is written for one: setup_inputs(seed, part) draws one part's arguments, and reference() takes and returns one part's arrays. A program takes and returns all parts, laid end to end along the dimension named above; an argument that names none is the same for every part. Nothing has to cross between parts.
All inputs are finite; a program needn't handle non-finite values.
Results may differ from the reference program's by a relative error of at most 0.0019.
Values may be sent and summed in bfloat16 or wider, within the bound.
No kernel may reach another device: no remote copies, remote signals or barrier semaphores. Data moves between devices by JAX's collectives and lax.ppermute only.
A program may use at most 448 MiB of HBM per device.

```python
import math
import jax
import jax.numpy as jnp
from jax import lax

NX = 256
NY = 256
COILS = 32
CH = 16
P_SIZE = 16


def plant(drawn, stream_key, smallest, top_value):
    extent = drawn.shape
    spot = [jax.random.randint(jax.random.fold_in(stream_key, axis), (), 0, extent[axis]) for axis in range(len(extent))]
    drawn = drawn.at[tuple(spot)].set(smallest)
    longest = extent.index(max(extent))
    spot[longest] = (spot[longest] + 1) % extent[longest]
    return drawn.at[tuple(spot)].set(top_value)


def with_spikes(entries, stream_key, source, target, blocks, factor):
    owner, partner = [(jnp.arange(entries.shape[dim]) // (entries.shape[dim] // blocks)).reshape([-1 if axis == dim else 1 for axis in range(entries.ndim)]) for dim in (source, target)]
    chosen = jax.random.permutation(stream_key, blocks)[partner]
    strong = (owner == chosen) | (owner == (partner + blocks // 2) % blocks)
    return jnp.where(strong, factor * entries, entries)


def steps_of(rng, extent, shards, smallest, top_value):
    loudness = 1.0
    for position, blocks in shards:
        heights = jax.random.uniform(jax.random.fold_in(jax.random.fold_in(rng, 6), position), (blocks,), jnp.float32, smallest / len(shards), top_value / len(shards))
        loudness = loudness * jnp.repeat(jnp.exp(heights), extent[position] // blocks).reshape((-1,) + (1,) * (len(extent) - 1 - position))
    return loudness


def bell_draw(key, shape, scale, reach, pieces=(), kind=jnp.bfloat16):
    array = jax.random.normal(key, shape, jnp.float32) * scale
    if len(pieces) > 0:
        array = steps_of(key, shape, pieces, -0.22, 0.18) * array
    return jnp.clip(array, min=-reach, max=reach).astype(kind)


def heavy_noise(key, shape, spread, limit, pieces, heavy, held_as=jnp.bfloat16):
    drawn = spread * jax.random.normal(key, shape, jnp.float32)
    if pieces:
        drawn = drawn * steps_of(key, shape, pieces, -0.22, 0.18)
    return jnp.clip(with_spikes(drawn, jax.random.fold_in(key, 3), *heavy), -limit, limit).astype(held_as)


def setup_inputs(seed: int = 0, part: int = 0) -> dict:
    splits = jax.random.split(jax.random.key(seed), 8)
    own_keys = jax.random.split(jax.random.fold_in(splits[7], part), 8)
    estimate = bell_draw(own_keys[0], (P_SIZE, NX, 2 * NY), 1.0, 6.0, ((0, 16),), jnp.float32)
    kdata = heavy_noise(own_keys[1], (P_SIZE, COILS, NX, 2 * NY), 0.5, 4.0, ((1, 16),), (1, 0, 16, 2.0), jnp.float32)
    maps = bell_draw(own_keys[2], (COILS, NX, 2 * NY), 0.125, 1.0, ((0, 16),), jnp.float32)
    mask = plant((jax.random.randint(own_keys[3], (P_SIZE, NY), 0, 3) < 1).astype(jnp.int32), jax.random.fold_in(own_keys[3], 1), 0, 1)
    w_first = bell_draw(splits[4], (CH, 2, 3, 3, 3), 54 ** -0.5, 0.875)
    w_middle = bell_draw(splits[5], (CH, CH, 3, 3, 3), (27 * CH) ** -0.5, 0.3125)
    w_last = bell_draw(splits[6], (2, CH, 3, 3, 3), (27 * CH) ** -0.5, 0.3125)
    return dict(estimate=estimate, kdata=kdata, maps=maps, mask=mask, w_first=w_first, w_middle=w_middle, w_last=w_last)


STEP_SIZE = 0.5
WEIGHT_RED = 0.5

def dft_tables(length, sign):
    index = jnp.arange(length, dtype=jnp.int32)
    product = index[:, None] * index[None, :] % length
    angle = product.astype(jnp.float32) * (2.0 * math.pi / length)
    scale = 1.0 / math.sqrt(length)
    return (jnp.cos(angle) * scale, -sign * jnp.sin(angle) * scale)

def row_matrix(length, sign):
    real_part, imag_part = dft_tables(length, sign)
    upper = jnp.concatenate([real_part, imag_part], 1)
    lower = jnp.concatenate([-imag_part, real_part], 1)
    return jnp.concatenate([upper, lower], 0).astype(jnp.bfloat16)

def column_matrix(length, sign):
    real_part, imag_part = dft_tables(length, sign)
    return jnp.concatenate([real_part, imag_part], 0).astype(jnp.bfloat16)

def combine_rows(both, rows, width):
    upper = both[:, :rows]
    lower = both[:, rows:]
    return upper + jnp.concatenate([-lower[..., width:], lower[..., :width]], -1)

def coil_term(image, sens, data, mask_wide, tables):
    row_fwd, col_fwd, row_inv, col_inv = tables
    count, rows, wide = image.shape
    width = wide // 2
    xf = image.astype(jnp.float32)
    xr, xi = (xf[..., :width], xf[..., width:])
    sr, si = (sens[..., :width], sens[..., width:])
    coil = jnp.concatenate([sr * xr - si * xi, sr * xi + si * xr], -1).astype(jnp.bfloat16)
    half = jnp.dot(coil.reshape(-1, wide), row_fwd, preferred_element_type=jnp.float32)
    half = half.reshape(count, rows, wide).astype(jnp.bfloat16)
    both = jnp.einsum('ux,pxk->puk', col_fwd.astype(jnp.float32), half.astype(jnp.float32))
    kspace = combine_rows(both, rows, width)
    resid = (mask_wide[:, None, :] * (kspace - data)).astype(jnp.bfloat16)
    both = jnp.einsum('ux,pxk->puk', col_inv.astype(jnp.float32), resid.astype(jnp.float32))
    back_half = combine_rows(both, rows, width).astype(jnp.bfloat16)
    back = jnp.dot(back_half.reshape(-1, wide), row_inv, preferred_element_type=jnp.float32)
    back = back.reshape(count, rows, wide)
    br, bi = (back[..., :width], back[..., width:])
    return jnp.concatenate([sr * br + si * bi, sr * bi - si * br], -1)

def conv_cyclic(values, weight):
    phases = values.shape[0]
    rows, width = (values.shape[2], values.shape[3])
    cin = values.shape[1]
    cout = weight.shape[0]
    extended = jnp.concatenate([values[-1:], values, values[:1]], 0)
    padded = jnp.pad(extended, ((0, 0), (0, 0), (1, 1), (1, 1)))
    folded = jnp.transpose(weight, (2, 0, 3, 4, 1)).reshape(3, cout, 9 * cin).astype(jnp.float32)

    def one_phase(index):
        window = lax.dynamic_slice_in_dim(padded, index, 3, 0)
        stacked = jnp.concatenate([window[:, :, a:a + rows, b:b + width] for a in range(3) for b in range(3)], 1)
        stacked = stacked.astype(jnp.float32)
        return jnp.einsum('dok,dkxy->oxy', folded, stacked)
    return lax.map(one_phase, jnp.arange(phases, dtype=jnp.int32))

def reference(estimate, kdata, maps, mask, w_first, w_middle, w_last):
    phases, rows, wide = estimate.shape
    width = wide // 2
    image = estimate.astype(jnp.bfloat16)
    tables = (row_matrix(width, 1.0), column_matrix(rows, 1.0), row_matrix(width, -1.0), column_matrix(rows, -1.0))
    mask_float = mask.astype(jnp.float32)
    mask_wide = jnp.concatenate([mask_float, mask_float], -1)

    def add_coil(index, total):
        sens = lax.dynamic_index_in_dim(maps, index, 0, keepdims=False)
        data = lax.dynamic_index_in_dim(kdata, index, 1, keepdims=False)
        return total + coil_term(image, sens, data, mask_wide, tables)
    grad = lax.fori_loop(0, kdata.shape[1], add_coil, jnp.zeros(estimate.shape, jnp.float32))
    channels = jnp.stack([image[..., :width], image[..., width:]], 1)
    first = jax.nn.relu(conv_cyclic(channels, w_first)).astype(jnp.bfloat16)
    second = jax.nn.relu(conv_cyclic(first, w_middle)).astype(jnp.bfloat16)
    noise = conv_cyclic(second, w_last)
    noise = jnp.concatenate([noise[:, 0], noise[:, 1]], -1)
    return estimate - STEP_SIZE * (grad + WEIGHT_RED * noise)
```

```python
import functools
import math

import jax
import jax.numpy as jnp
import numpy as np
from jax import lax
from jax.experimental import pallas as pl
from jax.experimental.pallas import tpu as pltpu
from jax.sharding import PartitionSpec as P

STEP_SIZE = 0.5
WEIGHT_RED = 0.5
BF = jnp.bfloat16
F32 = jnp.float32
LANE_BLOCKS = 4
VMEM_LIMIT = 56 * 1024 * 1024


def trig(rows, cols, length):
    angle = (rows[:, None] * cols[None, :] % length) * (2.0 * math.pi / length)
    scale = 1.0 / math.sqrt(length)
    return np.cos(angle) * scale, np.sin(angle) * scale


def as_bf16(table):
    return jnp.asarray(table.astype(np.float32)).astype(BF)


def left_tables(length):
    half = np.arange(length // 2)
    tables = []
    for parity in (0, 1):
        c, s = trig(half, 2 * half + parity, length)
        tables.append(np.block([[c, -s], [s, c]]))
    return as_bf16(np.stack(tables))


def right_inverse(length):
    full = np.arange(length)
    c, s = trig(full, full, length)
    return as_bf16(np.block([[c, s], [-s, c]]))


def projector_tables(length):
    half = np.arange(length // 2)
    first, second = [], []
    for parity in (0, 1):
        c, s = trig(half, 2 * half + parity, length)
        first.append(np.block([[c, -s], [s, c]]))
        second.append(np.block([[c.T, s.T], [-s.T, c.T]]))
    return as_bf16(np.stack(first)), as_bf16(np.stack(second))


def dot(a, b):
    return jnp.dot(a, b, preferred_element_type=F32)


def data_kernel(ids, *refs):
    kd = refs[:LANE_BLOCKS]
    maps, mask_wide, mask_par, left, right, first, second, out, proj = refs[LANE_BLOCKS:]
    coils, rows, wide = maps.shape
    width, half = wide // 2, rows // 2
    for e in range(2):
        lhs = first[e] * mask_par[0, e : e + 1].astype(BF)
        proj[0, e] = dot(lhs, second[e]).astype(BF)
    keep = mask_wide[0].astype(BF)
    total = None
    for c in range(coils):
        parts = []
        for e in range(2):
            lines = [part[0, c, pl.ds(e, half, stride=2), :].astype(BF) for part in kd]
            real, imag = lines[: LANE_BLOCKS // 2], lines[LANE_BLOCKS // 2 :]
            stacked = jnp.concatenate([jnp.concatenate(real, 1), jnp.concatenate(imag, 1)], 0)
            parts.append(dot(left[e], stacked))
        upper, lower = parts[0] + parts[1], parts[0] - parts[1]
        real = jnp.concatenate([upper[:half], lower[:half]], 0).astype(BF)
        imag = jnp.concatenate([upper[half:], lower[half:]], 0).astype(BF)
        back = dot(jnp.concatenate([real, imag], 1) * keep, right[...])
        br, bi = back[:, :width], back[:, width:]
        sr, si = maps[c, :, :width], maps[c, :, width:]
        term = (sr * br + si * bi, sr * bi - si * br)
        total = term if total is None else (total[0] + term[0], total[1] + term[1])
    out[0, :, :width] = total[0]
    out[0, :, width:] = total[1]


def data_term(ids, kdata, maps, mask_wide, mask_par, tables):
    left, right, first, second = tables
    phases, coils, rows, wide = kdata.shape
    count = ids.shape[0]
    whole = lambda a: pl.BlockSpec(a.shape, lambda i, ids: (0,) * a.ndim)
    lanes = wide // LANE_BLOCKS
    block = lambda q: pl.BlockSpec((1, coils, rows, lanes), lambda i, ids: (ids[i], 0, 0, q))
    return pl.pallas_call(
        data_kernel,
        grid_spec=pltpu.PrefetchScalarGridSpec(
            num_scalar_prefetch=1,
            grid=(count,),
            in_specs=[
                *[block(q) for q in range(LANE_BLOCKS)],
                whole(maps),
                pl.BlockSpec((1, 1, wide), lambda i, ids: (ids[i], 0, 0)),
                pl.BlockSpec((1, 2, wide // 2), lambda i, ids: (ids[i], 0, 0)),
                whole(left),
                whole(right),
                whole(first),
                whole(second),
            ],
            out_specs=[
                pl.BlockSpec((1, rows, wide), lambda i, ids: (i, 0, 0)),
                pl.BlockSpec((1, 2, wide // 2, wide // 2), lambda i, ids: (i, 0, 0, 0)),
            ],
        ),
        out_shape=[
            jax.ShapeDtypeStruct((count, rows, wide), F32),
            jax.ShapeDtypeStruct((count, 2, wide // 2, wide // 2), BF),
        ],
        compiler_params=pltpu.CompilerParams(vmem_limit_bytes=VMEM_LIMIT),
        cost_estimate=pl.CostEstimate(
            flops=count * coils * 12 * rows * (wide // 2) ** 2,
            bytes_accessed=count * coils * rows * wide * 4,
            transcendentals=0,
        ),
        name="data_term",
    )(ids, *[kdata] * LANE_BLOCKS, maps, mask_wide, mask_par, left, right, first, second)


def image_kernel(ids, place, xz, xy, xc, maps, data, proj, noise, away, mine, held):
    step = pl.program_id(0)
    coils, rows, wide = maps.shape
    width, quarter = wide // 2, wide // 4
    strip = noise.shape[1]

    @pl.when(step < 2)
    def _():
        held[...] = xc[jnp.minimum(step, 1)]

    @pl.when(step == 2)
    def _():
        held[...] = xz[0]

    @pl.when(step == 3)
    def _():
        held[...] = xy[0]

    xr = held[:, :width].astype(F32)
    xi = held[:, width:].astype(F32)
    real, imag = -data[0, :, :width], -data[0, :, width:]
    for c in range(coils):
        sr, si = maps[c, :, :width], maps[c, :, width:]
        cr, ci = sr * xr - si * xi, sr * xi + si * xr
        plus = jnp.concatenate(
            [cr[:, :quarter] + cr[:, quarter:], ci[:, :quarter] + ci[:, quarter:]], 1
        )
        minus = jnp.concatenate(
            [cr[:, :quarter] - cr[:, quarter:], ci[:, :quarter] - ci[:, quarter:]], 1
        )
        even = dot(plus.astype(BF), proj[0, 0])
        odd = dot(minus.astype(BF), proj[0, 1])
        low, high = even + odd, even - odd
        br = jnp.concatenate([low[:, :quarter], high[:, :quarter]], 1)
        bi = jnp.concatenate([low[:, quarter:], high[:, quarter:]], 1)
        real = real + sr * br + si * bi
        imag = imag + sr * bi - si * br
    held[:, :width] = real.astype(BF)
    held[:, width:] = imag.astype(BF)
    at = pl.ds(pl.multiple_of(place[0], strip), strip)
    held[at, :] = (held[at, :].astype(F32) + WEIGHT_RED * noise[0]).astype(BF)

    @pl.when(step < 2)
    def _():
        away[0] = held[...]

    @pl.when(step >= 2)
    def _():
        mine[0] = held[...]


def image_term(ids, place, xz, xy, xc, maps, data, proj, noise):
    coils, rows, wide = maps.shape
    strip = noise.shape[1]
    whole = lambda a: pl.BlockSpec(a.shape, lambda i, ids, place: (0,) * a.ndim)
    return pl.pallas_call(
        image_kernel,
        grid_spec=pltpu.PrefetchScalarGridSpec(
            num_scalar_prefetch=2,
            grid=(4,),
            in_specs=[
                whole(xz),
                whole(xy),
                whole(xc),
                whole(maps),
                pl.BlockSpec((1, rows, wide), lambda i, ids, place: (i, 0, 0)),
                pl.BlockSpec((1, 2, wide // 2, wide // 2), lambda i, ids, place: (i, 0, 0, 0)),
                pl.BlockSpec((1, strip, wide), lambda i, ids, place: (ids[i], 0, 0)),
            ],
            out_specs=[
                pl.BlockSpec((1, rows, wide), lambda i, ids, place: (jnp.minimum(i, 1), 0, 0)),
                pl.BlockSpec((1, rows, wide), lambda i, ids, place: (jnp.maximum(i - 2, 0), 0, 0)),
            ],
            scratch_shapes=[pltpu.VMEM((rows, wide), BF)],
        ),
        out_shape=[jax.ShapeDtypeStruct((2, rows, wide), BF)] * 2,
        compiler_params=pltpu.CompilerParams(vmem_limit_bytes=VMEM_LIMIT),
        cost_estimate=pl.CostEstimate(
            flops=4 * coils * 4 * rows * (wide // 2) ** 2,
            bytes_accessed=4 * rows * wide * 8,
            transcendentals=0,
        ),
        name="image_term",
    )(ids, place, xz, xy, xc, maps, data, proj, noise)


def shifted(value, step):
    if step == 1:
        return value
    width = value.shape[1]
    lane = lax.broadcasted_iota(jnp.int32, value.shape, 1)
    if step == 0:
        return jnp.where(lane == 0, 0.0, pltpu.roll(value, 1, 1))
    return jnp.where(lane == width - 1, 0.0, pltpu.roll(value, width - 1, 1))


def conv_kernel(ch, strips, a1, a2, a3, valid1, valid2, out, x1, h1, noise):
    phases, tall, wide = strips.shape
    width = wide // 2
    strip = tall - 8
    n2 = (strip + 2) // 2

    def load(p, carry):
        image = strips[p].astype(F32)
        both = jnp.concatenate([image[:, :width], image[:, width:]], 0)
        for f in range(3):
            x1[p + 1, f * 2 * tall : (f + 1) * 2 * tall] = shifted(both, f).astype(BF)
        return carry

    lax.fori_loop(0, phases, load, 0)
    x1[0] = x1[phases]
    x1[phases + 1] = x1[1]

    def first(p, carry):
        stacked = x1[pl.ds(p, 3)].reshape(18 * tall, width)
        value = jnp.maximum(dot(a1[...], stacked), 0.0) * valid1[...]
        for f in range(3):
            h1[p + 1, f] = shifted(value, f).astype(BF)
        return carry

    lax.fori_loop(0, phases, first, 0)
    h1[0] = h1[phases]
    h1[phases + 1] = h1[1]
    noise[...] = jnp.zeros_like(noise)

    def second(p, carry):
        blocks = []
        for b in range(2):
            lo = b * n2 * ch
            stacked = h1[pl.ds(p, 3), :, lo : lo + (n2 + 2) * ch, :]
            stacked = stacked.reshape(9 * (n2 + 2) * ch, width)
            blocks.append(dot(a2[...], stacked))
        value = jnp.maximum(jnp.concatenate(blocks, 0), 0.0) * valid2[...]
        spread = dot(a3[...], value.astype(BF))
        for d in range(3):
            part = None
            for f in range(3):
                lo = (d * 3 + f) * 2 * strip
                piece = shifted(spread[lo : lo + 2 * strip], f)
                part = piece if part is None else part + piece
            noise[p + 2 - d] += part
        return carry

    lax.fori_loop(0, phases, second, 0)
    noise[phases] += noise[0]
    noise[1] += noise[phases + 1]

    def store(p, carry):
        both = noise[p + 1]
        out[p, :, :width] = both[:strip]
        out[p, :, width:] = both[strip:]
        return carry

    lax.fori_loop(0, phases, store, 0)


def band(weight, outs, ins, offset):
    moved = jnp.transpose(weight, (0, 2, 4, 1, 3))
    zero = ((0, 0),) * 4
    rows = [
        jnp.pad(moved, zero + ((r + offset, ins - 3 - r - offset),)) for r in range(outs)
    ]
    return jnp.stack(rows)


def denoise(strips, w_first, w_middle, w_last, place, image_rows):
    phases, tall, wide = strips.shape
    strip, width, ch = tall - 8, wide // 2, w_first.shape[0]
    n2 = (strip + 2) // 2
    a1 = band(w_first, strip + 4, tall, 1).reshape((strip + 4) * ch, 18 * tall)
    a2 = jnp.swapaxes(band(w_middle, n2, n2 + 2, 0), 4, 5).reshape(n2 * ch, 9 * (n2 + 2) * ch)
    a3 = jnp.transpose(band(w_last, strip, strip + 2, 0), (2, 3, 1, 0, 5, 4))
    a3 = a3.reshape(18 * strip, (strip + 2) * ch)
    row1 = place - 2 + jnp.arange((strip + 4) * ch) // ch
    row2 = place - 1 + jnp.arange((strip + 2) * ch) // ch
    valid1 = ((row1 >= 0) & (row1 < image_rows)).astype(F32)[:, None]
    valid2 = ((row2 >= 0) & (row2 < image_rows)).astype(F32)[:, None]
    return pl.pallas_call(
        functools.partial(conv_kernel, ch),
        out_shape=jax.ShapeDtypeStruct((phases, strip, wide), F32),
        scratch_shapes=[
            pltpu.VMEM((phases + 2, 6 * tall, width), BF),
            pltpu.VMEM((phases + 2, 3, (strip + 4) * ch, width), BF),
            pltpu.VMEM((phases + 2, 2 * strip, width), F32),
        ],
        compiler_params=pltpu.CompilerParams(vmem_limit_bytes=VMEM_LIMIT),
        cost_estimate=pl.CostEstimate(
            flops=phases * 2 * width * (a1.size + 2 * a2.size + a3.size),
            bytes_accessed=phases * tall * wide * 6,
            transcendentals=0,
        ),
        name="denoise",
    )(strips, a1, a2, a3, valid1, valid2)


def shards(estimate, kdata, maps, mask, w_first, w_middle, w_last):
    count = lax.axis_size("phase")
    me = lax.axis_index("phase")
    planes = count // 4
    rows, wide = estimate.shape[1:]
    strip = rows // count
    image = estimate.astype(BF)
    tables = (left_tables(rows), right_inverse(wide // 2)) + projector_tables(wide // 2)
    mask_float = mask.astype(F32)
    mask_wide = jnp.concatenate([mask_float, mask_float], -1)[:, None]
    pairs = jnp.stack([mask_float[:, 0::2], mask_float[:, 1::2]], 1)
    mask_par = jnp.concatenate([pairs, pairs], -1)
    place = (me * strip).astype(jnp.int32)

    def send(value, shift=0, flip=0):
        pairs = [(i, ((i ^ flip) + 4 * shift) % count) for i in range(count)]
        return lax.ppermute(value, "phase", pairs)

    padded = jnp.pad(image[0], ((4, 4), (0, 0)))
    strips = jnp.stack([padded[strip * j : strip * j + strip + 8] for j in range(count)])
    strips = lax.all_to_all(strips, "phase", 0, 0, tiled=True)

    order = [k for k in (2, 1, planes - 1) if 0 < k < planes]
    order = list(dict.fromkeys(order + list(range(1, planes)) + [0]))
    images = {}
    for k in order:
        xz = image if k == 0 else send(image, shift=planes - k)
        xy = send(xz, flip=2)
        xc = send(jnp.concatenate([xz, xy]), flip=1)
        images[k] = (xz, xy, xc)

    noise = denoise(strips, w_first, w_middle, w_last, place, rows)
    flips = jnp.array([1, 3, 0, 2], jnp.int32)
    terms = {}
    for k in order:
        ids = ((me ^ flips) + 4 * k) % count
        terms[k] = (ids,) + tuple(data_term(ids, kdata, maps, mask_wide, mask_par, tables))

    total = None
    for k in order:
        ids, data, proj = terms[k]
        away, mine = image_term(ids, place[None], *images[k], maps, data, proj, noise)
        got = send(away, flip=1)
        pair = mine.astype(F32) + got.astype(F32)
        other = send(pair[1].astype(BF), flip=2)
        plane = pair[0] + other.astype(F32)
        if k:
            plane = send(plane.astype(BF), shift=k).astype(F32)
        total = plane if total is None else total + plane
    return estimate - STEP_SIZE * total[None]


def solution(mesh):
    return jax.shard_map(
        shards,
        mesh=mesh,
        in_specs=(
            P(("slab", "phase"), None, None),
            P("slab", "phase", None, None),
            P(("slab", "phase"), None, None),
            P("slab", None),
            P(),
            P(),
            P(),
        ),
        out_specs=P(("slab", "phase"), None, None),
        check_vma=False,
    )
```

```python
import functools
import math

import jax
import jax.numpy as jnp
import numpy as np
from jax import lax
from jax.experimental import pallas as pl
from jax.experimental.pallas import tpu as pltpu
from jax.sharding import PartitionSpec as P

STEP_SIZE = 0.5
WEIGHT_RED = 0.5
BF = jnp.bfloat16
F32 = jnp.float32
LANE_BLOCKS = 4
VMEM_LIMIT = 56 * 1024 * 1024


def trig(rows, cols, length):
    angle = (rows[:, None] * cols[None, :] % length) * (2.0 * math.pi / length)
    scale = 1.0 / math.sqrt(length)
    return np.cos(angle) * scale, np.sin(angle) * scale


def as_bf16(table):
    return jnp.asarray(table.astype(np.float32)).astype(BF)


def left_tables(length):
    half = np.arange(length // 2)
    tables = []
    for parity in (0, 1):
        c, s = trig(half, 2 * half + parity, length)
        tables.append(np.block([[c, -s], [s, c]]))
    return as_bf16(np.stack(tables))


def right_inverse(length):
    full = np.arange(length)
    c, s = trig(full, full, length)
    return as_bf16(np.block([[c, s], [-s, c]]))


def projector_tables(length):
    half = np.arange(length // 2)
    first, second = [], []
    for parity in (0, 1):
        c, s = trig(half, 2 * half + parity, length)
        first.append(np.block([[c, -s], [s, c]]))
        second.append(np.block([[c.T, s.T], [-s.T, c.T]]))
    return as_bf16(np.stack(first)), as_bf16(np.stack(second))


def cost(micros):
    return pl.CostEstimate(flops=int(micros * 1.0e9), bytes_accessed=0, transcendentals=0)


def dot(a, b):
    return jnp.dot(a, b, preferred_element_type=F32)


def data_kernel(group, ids, *refs):
    count = group * LANE_BLOCKS
    maps, left, right, first, second = refs[count : count + 5]
    masks = refs[count + 5 : count + 5 + group]
    out, proj = refs[count + 5 + group :]
    coils, rows, wide = maps.shape
    width, half = wide // 2, rows // 2
    for g in range(group):
        kd = refs[g * LANE_BLOCKS : (g + 1) * LANE_BLOCKS]
        mask = masks[g][0].astype(BF)
        keep = mask[:, :wide]
        masked = []
        for c in range(coils):
            parts = []
            for e in range(2):
                lines = [part[0, c, pl.ds(e, half, stride=2), :].astype(BF) for part in kd]
                real, imag = lines[: LANE_BLOCKS // 2], lines[LANE_BLOCKS // 2 :]
                stacked = jnp.concatenate([jnp.concatenate(real, 1), jnp.concatenate(imag, 1)], 0)
                parts.append(dot(left[e], stacked))
            upper, lower = parts[0] + parts[1], parts[0] - parts[1]
            real = jnp.concatenate([upper[:half], lower[:half]], 0).astype(BF)
            imag = jnp.concatenate([upper[half:], lower[half:]], 0).astype(BF)
            masked.append(jnp.concatenate([real, imag], 1) * keep)
        back = dot(jnp.concatenate(masked, 0), right[...])
        for e in range(2):
            lhs = first[e] * mask[:, wide + e * width : wide + (e + 1) * width]
            proj[g, e] = dot(lhs, second[e]).astype(BF)
        real, imag = None, None
        for c in range(coils):
            br, bi = back[c * rows : (c + 1) * rows, :width], back[c * rows : (c + 1) * rows, width:]
            sr, si = maps[c, :, :width], maps[c, :, width:]
            tr, ti = sr * br + si * bi, sr * bi - si * br
            real, imag = (tr, ti) if real is None else (real + tr, imag + ti)
        out[g, :, :width] = real.astype(BF)
        out[g, :, width:] = imag.astype(BF)


def data_term(ids, kdata, maps, masks, tables, group=2):
    phases, coils, rows, wide = kdata.shape
    count = ids.shape[0]
    lanes = wide // LANE_BLOCKS
    whole = lambda a: pl.BlockSpec(a.shape, lambda i, ids: (0,) * a.ndim)
    lines = lambda g, q: pl.BlockSpec(
        (1, coils, rows, lanes), lambda i, ids: (ids[group * i + g], 0, 0, q)
    )
    row = lambda g: pl.BlockSpec(
        (1,) + masks.shape[1:], lambda i, ids: (ids[group * i + g], 0, 0)
    )
    return pl.pallas_call(
        functools.partial(data_kernel, group),
        grid_spec=pltpu.PrefetchScalarGridSpec(
            num_scalar_prefetch=1,
            grid=(count // group,),
            in_specs=[lines(g, q) for g in range(group) for q in range(LANE_BLOCKS)]
            + [whole(a) for a in (maps,) + tables]
            + [row(g) for g in range(group)],
            out_specs=[
                pl.BlockSpec((group, rows, wide), lambda i, ids: (i, 0, 0)),
                pl.BlockSpec((group, 2, wide // 2, wide // 2), lambda i, ids: (i, 0, 0, 0)),
            ],
        ),
        out_shape=[
            jax.ShapeDtypeStruct((count, rows, wide), BF),
            jax.ShapeDtypeStruct((count, 2, wide // 2, wide // 2), BF),
        ],
        compiler_params=pltpu.CompilerParams(vmem_limit_bytes=VMEM_LIMIT),
        cost_estimate=cost(1.1 * count),
        name="data_term",
    )(ids, *[kdata] * (group * LANE_BLOCKS), maps, *tables, *[masks] * group)


def image_kernel(ids, place, far, near, maps, data, proj, noise_a, noise_b, away, mine, held):
    step = pl.program_id(0)
    coils, rows, wide = maps.shape
    width, quarter = wide // 2, wide // 4
    strip = noise_a.shape[1]

    @pl.when(step == 0)
    def _():
        held[...] = far[...]

    @pl.when(step == 1)
    def _():
        held[...] = near[...]

    at = pl.ds(pl.multiple_of(place[0], strip), strip)
    for g, noise in enumerate((noise_a, noise_b)):
        xr = held[g, :, :width].astype(F32)
        xi = held[g, :, width:].astype(F32)
        plus, minus = [], []
        for c in range(coils):
            sr, si = maps[c, :, :width], maps[c, :, width:]
            cr, ci = sr * xr - si * xi, sr * xi + si * xr
            cr0, cr1, ci0, ci1 = cr[:, :quarter], cr[:, quarter:], ci[:, :quarter], ci[:, quarter:]
            plus.append(jnp.concatenate([cr0 + cr1, ci0 + ci1], 1).astype(BF))
            minus.append(jnp.concatenate([cr0 - cr1, ci0 - ci1], 1).astype(BF))
        even = dot(jnp.concatenate(plus, 0), proj[g, 0])
        odd = dot(jnp.concatenate(minus, 0), proj[g, 1])
        real = -data[g, :, :width].astype(F32)
        imag = -data[g, :, width:].astype(F32)
        for c in range(coils):
            sr, si = maps[c, :, :width], maps[c, :, width:]
            p, q = even[c * rows : (c + 1) * rows], odd[c * rows : (c + 1) * rows]
            low, high = p + q, p - q
            br = jnp.concatenate([low[:, :quarter], high[:, :quarter]], 1)
            bi = jnp.concatenate([low[:, quarter:], high[:, quarter:]], 1)
            real = real + sr * br + si * bi
            imag = imag + sr * bi - si * br
        held[g, :, :width] = real.astype(BF)
        held[g, :, width:] = imag.astype(BF)
        held[g, at, :] = (held[g, at, :].astype(F32) + WEIGHT_RED * noise[0]).astype(BF)

    @pl.when(step == 0)
    def _():
        away[...] = held[...]

    @pl.when(step == 1)
    def _():
        mine[...] = held[...]


def image_term(ids, place, far, near, maps, data, proj, noise, chunk):
    coils, rows, wide = maps.shape
    strip, width = noise.shape[1], wide // 2
    whole = lambda a: pl.BlockSpec(a.shape, lambda i, ids, place: (0,) * a.ndim)
    extra = lambda g: pl.BlockSpec((1, strip, wide), lambda i, ids, place: (ids[2 * i + g], 0, 0))
    return pl.pallas_call(
        image_kernel,
        grid_spec=pltpu.PrefetchScalarGridSpec(
            num_scalar_prefetch=2,
            grid=(2,),
            in_specs=[
                whole(far),
                whole(near),
                whole(maps),
                pl.BlockSpec((2, rows, wide), lambda i, ids, place: (2 * chunk + i, 0, 0)),
                pl.BlockSpec((2, 2, width, width), lambda i, ids, place: (2 * chunk + i, 0, 0, 0)),
                extra(0),
                extra(1),
            ],
            out_specs=[whole(far)] * 2,
            scratch_shapes=[pltpu.VMEM((2, rows, wide), BF)],
        ),
        out_shape=[jax.ShapeDtypeStruct((2, rows, wide), BF)] * 2,
        compiler_params=pltpu.CompilerParams(vmem_limit_bytes=VMEM_LIMIT),
        cost_estimate=cost(5.0),
        name="image_term",
    )(ids, place, far, near, maps, data, proj, noise, noise)


def shifted(value, step):
    if step == 1:
        return value
    width = value.shape[1]
    lane = lax.broadcasted_iota(jnp.int32, value.shape, 1)
    if step == 0:
        return jnp.where(lane == 0, 0.0, pltpu.roll(value, 1, 1))
    return jnp.where(lane == width - 1, 0.0, pltpu.roll(value, width - 1, 1))


def conv_kernel(ch, place, strips, w1, w2, w3, pick1, pick2, spread3, out, x1, h1, noise, a1, a2, a3):
    phases, tall, wide = strips.shape
    width = wide // 2
    strip = tall - 8
    n1, n2, n3 = strip + 4, (strip + 2) // 2, strip + 2
    image_rows = strip * phases
    top = jnp.where(place[0] == 0, 0.0, 1.0)
    bottom = jnp.where(place[0] + strip == image_rows, 0.0, 1.0)

    base = dot(w1[...], pick1[...])
    for j in range(n1):
        line = base if j == 0 else pltpu.roll(base, j, 1)
        a1[j * ch : (j + 1) * ch] = line[:, : a1.shape[1]].astype(BF)
    base = dot(w2[...], pick2[...])
    for j in range(n2):
        line = base if j == 0 else pltpu.roll(base, j * ch, 1)
        a2[j * ch : (j + 1) * ch] = line[:, : a2.shape[1]].astype(BF)
    base = dot(w3[...], spread3[...])
    row = lax.broadcasted_iota(jnp.int32, (strip, base.shape[1]), 0)
    lane = lax.broadcasted_iota(jnp.int32, (strip, base.shape[1]), 1)
    for k in range(18):
        line = None
        for e in range(3):
            inside = (lane >= (row + e) * ch) & (lane < (row + e + 1) * ch)
            part = jnp.where(inside, base[3 * k + e : 3 * k + e + 1], 0.0)
            line = part if line is None else line + part
        a3[k * strip : (k + 1) * strip] = line[:, : a3.shape[1]].astype(BF)

    def inside_rows(value, rows):
        edge = rows * ch
        middle = value[edge : value.shape[0] - edge]
        return jnp.concatenate([value[:edge] * top, middle, value[value.shape[0] - edge :] * bottom], 0)

    def load(p, carry):
        image = strips[p].astype(F32)
        both = jnp.concatenate([image[:, :width], image[:, width:]], 0)
        for f in range(3):
            x1[p + 1, f * 2 * tall : (f + 1) * 2 * tall] = shifted(both, f).astype(BF)
        return carry

    lax.fori_loop(0, phases, load, 0, unroll=4)
    x1[0] = x1[phases]
    x1[phases + 1] = x1[1]

    def first(p, carry):
        stacked = x1[pl.ds(p, 3)].reshape(18 * tall, width)
        value = inside_rows(jnp.maximum(dot(a1[...], stacked), 0.0), 2)
        for f in range(3):
            h1[p + 1, f] = shifted(value, f).astype(BF)
        return carry

    lax.fori_loop(0, phases, first, 0, unroll=16)
    h1[0] = h1[phases]
    h1[phases + 1] = h1[1]
    noise[...] = jnp.zeros_like(noise)

    def second(p, carry):
        blocks = []
        for b in range(2):
            lo = b * n2 * ch
            stacked = h1[pl.ds(p, 3), :, lo : lo + (n2 + 2) * ch, :]
            stacked = stacked.reshape(9 * (n2 + 2) * ch, width)
            blocks.append(dot(a2[...], stacked))
        value = inside_rows(jnp.maximum(jnp.concatenate(blocks, 0), 0.0), 1)
        spread = dot(a3[...], value.astype(BF))
        for d in range(3):
            part = None
            for f in range(3):
                lo = (d * 3 + f) * 2 * strip
                piece = shifted(spread[lo : lo + 2 * strip], f)
                part = piece if part is None else part + piece
            noise[p + 2 - d] += part
        return carry

    lax.fori_loop(0, phases, second, 0, unroll=16)
    noise[phases] += noise[0]
    noise[1] += noise[phases + 1]

    def store(p, carry):
        both = noise[p + 1]
        out[p, :, :width] = both[:strip]
        out[p, :, width:] = both[strip:]
        return carry

    lax.fori_loop(0, phases, store, 0, unroll=4)


def pick_tables(cin, tall, n2, ch, n3):
    pad = lambda n: -(-n // 128) * 128
    pick1 = np.zeros((cin * 27, pad(9 * cin * tall)), np.float32)
    pick2 = np.zeros((ch * 27, pad(9 * (n2 + 2) * ch)), np.float32)
    for d in range(3):
        for e in range(3):
            for f in range(3):
                tap = (d * 3 + e) * 3 + f
                for c in range(cin):
                    pick1[c * 27 + tap, ((d * 3 + f) * cin + c) * tall + 1 + e] = 1.0
                for c in range(ch):
                    pick2[c * 27 + tap, ((d * 3 + f) * (n2 + 2) + e) * ch + c] = 1.0
    spread3 = np.zeros((ch, pad(n3 * ch)), np.float32)
    for c in range(ch):
        spread3[c, c : n3 * ch : ch] = 1.0
    return as_bf16(pick1), as_bf16(pick2), as_bf16(spread3)


def denoise(strips, w_first, w_middle, w_last, place):
    phases, tall, wide = strips.shape
    strip, width, (ch, cin) = tall - 8, wide // 2, w_first.shape[:2]
    n1, n2, n3 = strip + 4, (strip + 2) // 2, strip + 2
    picks = pick_tables(cin, tall, n2, ch, n3)
    weights = (
        w_first.reshape(ch, cin * 27),
        w_middle.reshape(ch, ch * 27),
        jnp.transpose(w_last, (2, 4, 0, 3, 1)).reshape(54, ch),
    )
    vmem = pl.BlockSpec(memory_space=pltpu.VMEM)
    return pl.pallas_call(
        functools.partial(conv_kernel, ch),
        in_specs=[pl.BlockSpec(memory_space=pltpu.SMEM)] + [vmem] * 7,
        out_specs=vmem,
        out_shape=jax.ShapeDtypeStruct((phases, strip, wide), F32),
        scratch_shapes=[
            pltpu.VMEM((phases + 2, 6 * tall, width), BF),
            pltpu.VMEM((phases + 2, 3, n1 * ch, width), BF),
            pltpu.VMEM((phases + 2, 2 * strip, width), F32),
            pltpu.VMEM((n1 * ch, 9 * cin * tall), BF),
            pltpu.VMEM((n2 * ch, 9 * (n2 + 2) * ch), BF),
            pltpu.VMEM((18 * strip, n3 * ch), BF),
        ],
        compiler_params=pltpu.CompilerParams(vmem_limit_bytes=VMEM_LIMIT),
        cost_estimate=cost(13.0),
        name="denoise",
    )(place, strips, *weights, *picks)


def prepare_kernel(estimate, mask, pick, image, strips, masks, padded):
    rows, wide = estimate.shape[1:]
    phases, tall = strips.shape[:2]
    strip = tall - 8
    value = estimate[0]
    image[0] = value.astype(BF)
    edge = jnp.zeros((4, wide), F32)
    padded[0:4] = edge
    padded[rows + 4 : rows + 8] = edge
    padded[4 : rows + 4] = value
    for j in range(phases):
        strips[j] = padded[j * strip : j * strip + tall].astype(BF)
    spread = dot(mask[...].astype(F32).astype(BF), pick[...])
    for p in range(phases):
        masks[p] = spread[p : p + 1]


def prepare(estimate, mask):
    rows, wide = estimate.shape[1:]
    phases, width = mask.shape
    tall = rows // phases + 8
    pick = np.zeros((width, 4 * width), np.float32)
    half = width // 2
    for k in range(width):
        pick[k, [k, width + k]] = 1.0
        at = 2 * width + (k % 2) * width + k // 2
        pick[k, [at, at + half]] = 1.0
    return pl.pallas_call(
        prepare_kernel,
        out_shape=[
            jax.ShapeDtypeStruct((1, rows, wide), BF),
            jax.ShapeDtypeStruct((phases, tall, wide), BF),
            jax.ShapeDtypeStruct((phases, 1, 4 * width), F32),
        ],
        scratch_shapes=[pltpu.VMEM((rows + 8, wide), F32)],
        cost_estimate=cost(2.0),
        name="prepare",
    )(estimate, mask, as_bf16(pick))


def shards(estimate, kdata, maps, mask, w_first, w_middle, w_last):
    count = lax.axis_size("phase")
    me = lax.axis_index("phase")
    planes = count // 4
    rows, wide = estimate.shape[1:]
    strip = rows // count
    tables = (left_tables(rows), right_inverse(wide // 2)) + projector_tables(wide // 2)
    place = (me * strip).astype(jnp.int32)[None]

    def send(value, shift=0, flip=0):
        pairs = [(i, ((i ^ flip) + 4 * shift) % count) for i in range(count)]
        return lax.ppermute(value, "phase", pairs)

    image, strips, masks = prepare(estimate, mask)
    strips = lax.all_to_all(strips, "phase", 0, 0, tiled=True)

    order = [k for k in (2, 1, planes - 1) if 0 < k < planes]
    order = list(dict.fromkeys(order + list(range(1, planes)) + [0]))
    images = {}
    for k in order:
        xz = image if k == 0 else send(image, shift=planes - k)
        near = jnp.concatenate([xz, send(xz, flip=2)])
        images[k] = (send(near, flip=1), near)

    flips = jnp.array([1, 3, 0, 2], jnp.int32)
    ids = {k: ((me ^ flips) + 4 * k) % count for k in order}
    terms = {}
    for pair in [order[i : i + 2] for i in range(0, planes, 2)]:
        both = jnp.concatenate([ids[k] for k in pair])
        data, proj = data_term(both, kdata, maps, masks, tables)
        for n, k in enumerate(pair):
            terms[k] = (data, proj, n)

    noise = denoise(strips, w_first, w_middle, w_last, place)

    total = None
    for k in order:
        data, proj, n = terms[k]
        away, mine = image_term(ids[k], place, *images[k], maps, data, proj, noise, n)
        got = send(away, flip=1)
        pair = mine.astype(F32) + got.astype(F32)
        other = send(pair[1].astype(BF), flip=2)
        plane = pair[0] + other.astype(F32)
        if k:
            plane = send(plane.astype(BF), shift=k).astype(F32)
        total = plane if total is None else total + plane
    return estimate - STEP_SIZE * total[None]


def solution(mesh):
    return jax.shard_map(
        shards,
        mesh=mesh,
        in_specs=(
            P(("slab", "phase"), None, None),
            P("slab", "phase", None, None),
            P(("slab", "phase"), None, None),
            P("slab", None),
            P(),
            P(),
            P(),
        ),
        out_specs=P(("slab", "phase"), None, None),
        check_vma=False,
    )
```

```python
import functools
import math

import jax
import jax.numpy as jnp
import numpy as np
from jax import lax
from jax.experimental import pallas as pl
from jax.experimental.pallas import tpu as pltpu
from jax.sharding import PartitionSpec as P

STEP_SIZE = 0.5
WEIGHT_RED = 0.5
BF = jnp.bfloat16
F32 = jnp.float32
LANE_BLOCKS = 4
TILE = 32
MIB = 1024 * 1024


def trig(rows, cols, length):
    angle = (rows[:, None] * cols[None, :] % length) * (2.0 * math.pi / length)
    scale = 1.0 / math.sqrt(length)
    return np.cos(angle) * scale, np.sin(angle) * scale


def as_bf16(table):
    return jnp.asarray(table.astype(np.float32)).astype(BF)


def left_tables(length):
    half = np.arange(length // 2)
    tables = []
    for parity in (0, 1):
        c, s = trig(half, 2 * half + parity, length)
        tables.append(np.block([[c, -s], [s, c]]))
    return as_bf16(np.stack(tables))


def right_inverse(length):
    full = np.arange(length)
    c, s = trig(full, full, length)
    return as_bf16(np.block([[c, s], [-s, c]]))


def projector_tables(length):
    half = np.arange(length // 2)
    first, second = [], []
    for parity in (0, 1):
        c, s = trig(half, 2 * half + parity, length)
        first.append(np.block([[c, -s], [s, c]]))
        second.append(np.block([[c.T, s.T], [-s.T, c.T]]))
    return as_bf16(np.stack(first)), as_bf16(np.stack(second))


def cost(micros):
    return pl.CostEstimate(flops=int(micros * 1.0e9), bytes_accessed=0, transcendentals=0)


def dot(a, b):
    return jnp.dot(a, b, preferred_element_type=F32)


def joined(real, imag):
    return jnp.concatenate([real.astype(BF), imag.astype(BF)], 1)


def data_kernel(group, ids, *refs):
    count = group * LANE_BLOCKS
    refs = refs[: count + 5 + group] + refs[-2:]
    maps, left, right, first, second = refs[count : count + 5]
    masks = refs[count + 5 : count + 5 + group]
    out, proj = refs[count + 5 + group :]
    coils, rows, wide = maps.shape
    width, half = wide // 2, rows // 2
    for g in range(group):
        kd = refs[g * LANE_BLOCKS : (g + 1) * LANE_BLOCKS]
        mask = masks[g][0].astype(BF)
        keep = mask[:, :wide]
        masked = []
        for c in range(coils):
            parts = []
            for e in range(2):
                lines = [part[0, c, pl.ds(e, half, stride=2), :].astype(BF) for part in kd]
                real, imag = lines[: LANE_BLOCKS // 2], lines[LANE_BLOCKS // 2 :]
                stacked = jnp.concatenate([jnp.concatenate(real, 1), jnp.concatenate(imag, 1)], 0)
                parts.append(dot(left[e], stacked))
            uppers, lowers = [], []
            for r in range(0, half, TILE):
                at, to = slice(r, r + TILE), slice(half + r, half + r + TILE)
                uppers.append(joined(parts[0][at] + parts[1][at], parts[0][to] + parts[1][to]) * keep)
                lowers.append(joined(parts[0][at] - parts[1][at], parts[0][to] - parts[1][to]) * keep)
            masked += uppers + lowers
        back = dot(jnp.concatenate(masked, 0), right[...])
        for e in range(2):
            lhs = first[e] * mask[:, wide + e * width : wide + (e + 1) * width]
            proj[g, e] = dot(lhs, second[e]).astype(BF)
        for r in range(0, rows, TILE):
            real, imag = None, None
            for c in range(coils):
                line = back[c * rows + r : c * rows + r + TILE]
                br, bi = line[:, :width], line[:, width:]
                sr, si = maps[c, r : r + TILE, :width], maps[c, r : r + TILE, width:]
                tr, ti = sr * br + si * bi, sr * bi - si * br
                real, imag = (tr, ti) if real is None else (real + tr, imag + ti)
            out[g, r : r + TILE] = joined(real, imag)


def data_term(ids, kdata, maps, masks, tables, after, group=2):
    phases, coils, rows, wide = kdata.shape
    count = ids.shape[0]
    lanes = wide // LANE_BLOCKS
    whole = lambda a: pl.BlockSpec(a.shape, lambda i, ids: (0,) * a.ndim)
    lines = lambda g, q: pl.BlockSpec(
        (1, coils, rows, lanes), lambda i, ids: (ids[group * i + g], 0, 0, q)
    )
    row = lambda g: pl.BlockSpec(
        (1,) + masks.shape[1:], lambda i, ids: (ids[group * i + g], 0, 0)
    )
    return pl.pallas_call(
        functools.partial(data_kernel, group),
        grid_spec=pltpu.PrefetchScalarGridSpec(
            num_scalar_prefetch=1,
            grid=(count // group,),
            in_specs=[lines(g, q) for g in range(group) for q in range(LANE_BLOCKS)]
            + [whole(a) for a in (maps,) + tables]
            + [row(g) for g in range(group)]
            + [pl.BlockSpec(memory_space=pl.ANY)] * len(after),
            out_specs=[
                pl.BlockSpec((group, rows, wide), lambda i, ids: (i, 0, 0)),
                pl.BlockSpec((group, 2, wide // 2, wide // 2), lambda i, ids: (i, 0, 0, 0)),
            ],
        ),
        out_shape=[
            jax.ShapeDtypeStruct((count, rows, wide), BF),
            jax.ShapeDtypeStruct((count, 2, wide // 2, wide // 2), BF),
        ],
        compiler_params=pltpu.CompilerParams(vmem_limit_bytes=24 * MIB),
        cost_estimate=cost(1.1 * count),
        name="data_term",
    )(ids, *[pltpu.with_memory_space_constraint(kdata, pltpu.HBM)] * (group * LANE_BLOCKS), maps, *tables, *[masks] * group, *after)


def image_kernel(ids, place, far_a, far_b, near_a, near_b, maps, data, proj, noise_a, noise_b, *rest):
    away, mine, held = rest[-3:]
    step = pl.program_id(0)
    coils, rows, wide = maps.shape
    width, quarter = wide // 2, wide // 4
    strip = noise_a.shape[1]

    @pl.when(step == 0)
    def _():
        held[0] = far_a[0]
        held[1] = far_b[0]

    @pl.when(step == 1)
    def _():
        held[0] = near_a[0]
        held[1] = near_b[0]

    at = pl.ds(pl.multiple_of(place[0], strip), strip)
    for g, noise in enumerate((noise_a, noise_b)):
        plus, minus = [], []
        for c in range(coils):
            for r in range(0, rows, TILE):
                to = slice(r, r + TILE)
                xr, xi = held[g, to, :width].astype(F32), held[g, to, width:].astype(F32)
                sr, si = maps[c, to, :width], maps[c, to, width:]
                cr, ci = sr * xr - si * xi, sr * xi + si * xr
                cr0, cr1, ci0, ci1 = cr[:, :quarter], cr[:, quarter:], ci[:, :quarter], ci[:, quarter:]
                plus.append(joined(cr0 + cr1, ci0 + ci1))
                minus.append(joined(cr0 - cr1, ci0 - ci1))
        even = dot(jnp.concatenate(plus, 0), proj[g, 0])
        odd = dot(jnp.concatenate(minus, 0), proj[g, 1])
        for r in range(0, rows, TILE):
            to = slice(r, r + TILE)
            real = -data[g, to, :width].astype(F32)
            imag = -data[g, to, width:].astype(F32)
            for c in range(coils):
                sr, si = maps[c, to, :width], maps[c, to, width:]
                p, q = even[c * rows + r : c * rows + r + TILE], odd[c * rows + r : c * rows + r + TILE]
                low, high = p + q, p - q
                br = jnp.concatenate([low[:, :quarter], high[:, :quarter]], 1)
                bi = jnp.concatenate([low[:, quarter:], high[:, quarter:]], 1)
                real = real + sr * br + si * bi
                imag = imag + sr * bi - si * br
            held[g, to, :] = joined(real, imag)
        held[g, at, :] = (held[g, at, :].astype(F32) + WEIGHT_RED * noise[0]).astype(BF)

    @pl.when(step == 0)
    def _():
        away[...] = held[...]

    @pl.when(step == 1)
    def _():
        mine[...] = held[...]


def image_term(ids, place, images, maps, data, proj, noise, chunk, after):
    coils, rows, wide = maps.shape
    strip, width = noise.shape[1], wide // 2
    whole = lambda a: pl.BlockSpec(a.shape, lambda i, ids, place: (0,) * a.ndim)
    extra = lambda g: pl.BlockSpec((1, strip, wide), lambda i, ids, place: (ids[2 * i + g], 0, 0))
    return pl.pallas_call(
        image_kernel,
        grid_spec=pltpu.PrefetchScalarGridSpec(
            num_scalar_prefetch=2,
            grid=(2,),
            in_specs=[
                *[whole(a) for a in images],
                whole(maps),
                pl.BlockSpec((2, rows, wide), lambda i, ids, place: (2 * chunk + i, 0, 0)),
                pl.BlockSpec((2, 2, width, width), lambda i, ids, place: (2 * chunk + i, 0, 0, 0)),
                extra(0),
                extra(1),
            ]
            + [pl.BlockSpec(memory_space=pl.ANY)] * len(after),
            out_specs=[pl.BlockSpec((2, rows, wide), lambda i, ids, place: (0, 0, 0))] * 2,
            scratch_shapes=[pltpu.VMEM((2, rows, wide), BF)],
        ),
        out_shape=[jax.ShapeDtypeStruct((2, rows, wide), BF)] * 2,
        compiler_params=pltpu.CompilerParams(vmem_limit_bytes=16 * MIB),
        cost_estimate=cost(5.0),
        name="image_term",
    )(ids, place, *images, maps, data, proj, noise, noise, *after)


def shifted(value, step):
    if step == 1:
        return value
    width = value.shape[1]
    lane = lax.broadcasted_iota(jnp.int32, value.shape, 1)
    if step == 0:
        return jnp.where(lane == 0, 0.0, pltpu.roll(value, 1, 1))
    return jnp.where(lane == width - 1, 0.0, pltpu.roll(value, width - 1, 1))


def conv_kernel(ch, place, strips, w1, w2, w3, pick1, pick2, spread3, *rest):
    out, x1, h1, noise, a1, a2, a3 = rest[-7:]
    phases, tall, wide = strips.shape
    width = wide // 2
    strip = tall - 8
    n1, n2, n3 = strip + 4, (strip + 2) // 2, strip + 2
    image_rows = strip * phases
    top = jnp.where(place[0] == 0, 0.0, 1.0)
    bottom = jnp.where(place[0] + strip == image_rows, 0.0, 1.0)

    base = None
    for tap in range(27):
        part = lax.dot_general(w1[tap], pick1[tap], (((0,), (0,)), ((), ())), preferred_element_type=F32)
        base = part if base is None else base + part
    for j in range(n1):
        line = base if j == 0 else pltpu.roll(base, j, 1)
        a1[j * ch : (j + 1) * ch] = line[:, : a1.shape[1]].astype(BF)
    tiles = [jnp.zeros((ch, 128), F32)] * (-(-a2.shape[1] // 128))
    for tap in range(27):
        d, e, f = tap // 9, tap // 3 % 3, tap % 3
        at = ((d * 3 + f) * (n2 + 2) + e) * ch
        tiles[at // 128] = tiles[at // 128] + dot(w2[tap], pick2[at % 128 // ch])
    base = jnp.concatenate(tiles, 1)
    for j in range(n2):
        line = base if j == 0 else pltpu.roll(base, j * ch, 1)
        a2[j * ch : (j + 1) * ch] = line[:, : a2.shape[1]].astype(BF)
    lines = [dot(w3[tap], spread3[...]) for tap in range(27)]
    row = lax.broadcasted_iota(jnp.int32, (strip, spread3.shape[1]), 0)
    lane = lax.broadcasted_iota(jnp.int32, (strip, spread3.shape[1]), 1)
    for k in range(18):
        line = None
        for e in range(3):
            inside = (lane >= (row + e) * ch) & (lane < (row + e + 1) * ch)
            d, f, o = k // 6, k // 2 % 3, k % 2
            part = jnp.where(inside, lines[(d * 3 + e) * 3 + f][o : o + 1], 0.0)
            line = part if line is None else line + part
        a3[k * strip : (k + 1) * strip] = line[:, : a3.shape[1]].astype(BF)

    def inside_rows(value, rows):
        edge = rows * ch
        middle = value[edge : value.shape[0] - edge]
        return jnp.concatenate([value[:edge] * top, middle, value[value.shape[0] - edge :] * bottom], 0)

    def load(p, carry):
        image = strips[p].astype(F32)
        both = jnp.concatenate([image[:, :width], image[:, width:]], 0)
        for f in range(3):
            x1[p + 1, f * 2 * tall : (f + 1) * 2 * tall] = shifted(both, f).astype(BF)
        return carry

    lax.fori_loop(0, phases, load, 0, unroll=4)
    x1[0] = x1[phases]
    x1[phases + 1] = x1[1]

    def first(p, carry):
        stacked = x1[pl.ds(p, 3)].reshape(18 * tall, width)
        value = inside_rows(jnp.maximum(dot(a1[...], stacked), 0.0), 2)
        for f in range(3):
            h1[p + 1, f] = shifted(value, f).astype(BF)
        return carry

    lax.fori_loop(0, phases, first, 0, unroll=16)
    h1[0] = h1[phases]
    h1[phases + 1] = h1[1]
    noise[...] = jnp.zeros_like(noise)

    def second(p, carry):
        blocks = []
        for b in range(2):
            lo = b * n2 * ch
            stacked = h1[pl.ds(p, 3), :, lo : lo + (n2 + 2) * ch, :]
            stacked = stacked.reshape(9 * (n2 + 2) * ch, width)
            blocks.append(dot(a2[...], stacked))
        value = inside_rows(jnp.maximum(jnp.concatenate(blocks, 0), 0.0), 1)
        spread = dot(a3[...], value.astype(BF))
        for d in range(3):
            part = None
            for f in range(3):
                lo = (d * 3 + f) * 2 * strip
                piece = shifted(spread[lo : lo + 2 * strip], f)
                part = piece if part is None else part + piece
            noise[p + 2 - d] += part
        return carry

    lax.fori_loop(0, phases, second, 0, unroll=16)
    noise[phases] += noise[0]
    noise[1] += noise[phases + 1]

    def store(p, carry):
        both = noise[p + 1]
        out[p, :, :width] = both[:strip]
        out[p, :, width:] = both[strip:]
        return carry

    lax.fori_loop(0, phases, store, 0, unroll=4)


def pick_tables(cin, tall, ch, n3):
    pad = lambda n: -(-n // 128) * 128
    pick1 = np.zeros((27, cin, pad(9 * cin * tall)), np.float32)
    for d in range(3):
        for e in range(3):
            for f in range(3):
                for c in range(cin):
                    pick1[(d * 3 + e) * 3 + f, c, ((d * 3 + f) * cin + c) * tall + 1 + e] = 1.0
    pick2 = np.zeros((128 // ch, ch, 128), np.float32)
    for slot in range(128 // ch):
        pick2[slot, :, slot * ch : (slot + 1) * ch] = np.eye(ch)
    spread3 = np.zeros((ch, pad(n3 * ch)), np.float32)
    for c in range(ch):
        spread3[c, c : n3 * ch : ch] = 1.0
    return as_bf16(pick1), as_bf16(pick2), as_bf16(spread3)


def denoise(strips, w_first, w_middle, w_last, place, after):
    phases, tall, wide = strips.shape
    strip, width, (ch, cin) = tall - 8, wide // 2, w_first.shape[:2]
    n1, n2, n3 = strip + 4, (strip + 2) // 2, strip + 2
    picks = pick_tables(cin, tall, ch, n3)
    weights = (
        jnp.transpose(w_first, (2, 3, 4, 1, 0)).reshape(27, cin, ch),
        jnp.transpose(w_middle, (2, 3, 4, 0, 1)).reshape(27, ch, ch),
        jnp.transpose(w_last, (2, 3, 4, 0, 1)).reshape(27, 2, ch),
    )
    vmem = pl.BlockSpec(memory_space=pltpu.VMEM)
    return pl.pallas_call(
        functools.partial(conv_kernel, ch),
        in_specs=[pl.BlockSpec(memory_space=pltpu.SMEM)]
        + [vmem] * 7
        + [pl.BlockSpec(memory_space=pl.ANY)] * len(after),
        out_specs=vmem,
        out_shape=jax.ShapeDtypeStruct((phases, strip, wide), F32),
        scratch_shapes=[
            pltpu.VMEM((phases + 2, 6 * tall, width), BF),
            pltpu.VMEM((phases + 2, 3, n1 * ch, width), BF),
            pltpu.VMEM((phases + 2, 2 * strip, width), F32),
            pltpu.VMEM((n1 * ch, 9 * cin * tall), BF),
            pltpu.VMEM((n2 * ch, 9 * (n2 + 2) * ch), BF),
            pltpu.VMEM((18 * strip, n3 * ch), BF),
        ],
        compiler_params=pltpu.CompilerParams(vmem_limit_bytes=20 * MIB),
        cost_estimate=cost(13.0),
        name="denoise",
    )(place, strips, *weights, *picks, *after)


def prepare_kernel(estimate, mask, pick, image, strips, masks, padded):
    rows, wide = estimate.shape[1:]
    phases, tall = strips.shape[:2]
    strip = tall - 8
    value = estimate[0]
    image[0] = value.astype(BF)
    edge = jnp.zeros((4, wide), F32)
    padded[0:4] = edge
    padded[rows + 4 : rows + 8] = edge
    padded[4 : rows + 4] = value
    for j in range(phases):
        strips[j] = padded[j * strip : j * strip + tall].astype(BF)
    spread = dot(mask[...].astype(F32).astype(BF), pick[...])
    for p in range(phases):
        masks[p] = spread[p : p + 1]


def prepare(estimate, mask):
    rows, wide = estimate.shape[1:]
    phases, width = mask.shape
    tall = rows // phases + 8
    pick = np.zeros((width, 4 * width), np.float32)
    half = width // 2
    for k in range(width):
        pick[k, [k, width + k]] = 1.0
        at = 2 * width + (k % 2) * width + k // 2
        pick[k, [at, at + half]] = 1.0
    return pl.pallas_call(
        prepare_kernel,
        out_shape=[
            jax.ShapeDtypeStruct((1, rows, wide), BF),
            jax.ShapeDtypeStruct((phases, tall, wide), BF),
            jax.ShapeDtypeStruct((phases, 1, 4 * width), F32),
        ],
        scratch_shapes=[pltpu.VMEM((rows + 8, wide), F32)],
        cost_estimate=cost(2.0),
        name="prepare",
    )(estimate, mask, as_bf16(pick))


def shards(estimate, kdata, maps, mask, w_first, w_middle, w_last):
    count = lax.axis_size("phase")
    me = lax.axis_index("phase")
    planes = count // 4
    rows, wide = estimate.shape[1:]
    strip = rows // count
    tables = (left_tables(rows), right_inverse(wide // 2)) + projector_tables(wide // 2)
    place = (me * strip).astype(jnp.int32)[None]

    def send(value, shift=0, flip=0):
        pairs = [(i, ((i ^ flip) + 4 * shift) % count) for i in range(count)]
        return lax.ppermute(value, "phase", pairs)

    def behind(value, *earlier):
        return lax.optimization_barrier((value,) + earlier)[0]

    order = list(dict.fromkeys([planes // 2, 0] + list(range(planes))))
    lead, rest = order[:2], order[2:]
    flips = jnp.array([1, 3, 0, 2], jnp.int32)
    ids = {k: ((me ^ flips) + 4 * k) % count for k in order}

    image, strips, masks = prepare(estimate, mask)
    own, across, images, terms = {0: image}, {}, {}, {}
    far = order[0]
    if far:
        own[far] = send(image, shift=planes - far)
    across[0] = send(image, flip=2)
    strips = lax.all_to_all(strips, "phase", 0, 0, tiled=True)

    def data_of(chunks, after):
        both = jnp.concatenate([ids[k] for k in chunks])
        data, proj = data_term(both, kdata, maps, masks, tables, after)
        for n, k in enumerate(chunks):
            terms[k] = (data, proj, n)
        return data

    def gather(k):
        images[k] = (send(own[k], flip=1), send(across[k], flip=1), own[k], across[k])

    pairs, planed = {}, {}

    def start(k, after):
        data, proj, n = terms[k]
        away, mine = image_term(ids[k], place, images[k], maps, data, proj, noise, n, after)
        pairs[k] = mine.astype(F32) + send(away, flip=1).astype(F32)

    def finish(k):
        plane = (pairs[k][0] + send(pairs[k][1].astype(BF), flip=2).astype(F32)).astype(BF)
        planed[k] = (plane, send(plane, shift=k) if k else plane)

    first = data_of(lead, ())
    gather(0)
    for k in rest:
        own[k] = send(behind(image, own[far]), shift=planes - k)
    if far:
        across[far] = send(own[far], flip=2)
    noise = denoise(strips, w_first, w_middle, w_last, place, (first, own[far], across[0]))
    if far:
        across[far] = behind(across[far], noise)
        gather(far)
    for k in rest:
        across[k] = send(own[k], flip=2)

    for k in lead:
        start(k, tuple(own[r] for r in rest))
        finish(k)
    after = tuple(pairs[k] for k in lead)
    if rest:
        data_of(rest, after + (noise,) + tuple(across[k] for k in rest))
    after = (planed[lead[0]][0],)
    for k in rest:
        gather(k)
    for k in rest:
        start(k, after)
        finish(k)
        after = (pairs[k],)
    total = sum(planed[k][1].astype(F32) for k in order)
    return estimate - STEP_SIZE * total[None]


def solution(mesh):
    return jax.shard_map(
        shards,
        mesh=mesh,
        in_specs=(
            P(("slab", "phase"), None, None),
            P("slab", "phase", None, None),
            P(("slab", "phase"), None, None),
            P("slab", None),
            P(),
            P(),
            P(),
        ),
        out_specs=P(("slab", "phase"), None, None),
        check_vma=False,
    )
```

```python
import functools
import math

import jax
import jax.numpy as jnp
import numpy as np
from jax import lax
from jax.experimental import pallas as pl
from jax.experimental.pallas import tpu as pltpu
from jax.sharding import PartitionSpec as P

STEP_SIZE = 0.5
WEIGHT_RED = 0.5
BF = jnp.bfloat16
F32 = jnp.float32
LANE_BLOCKS = 4
TILE = 32
MIB = 1024 * 1024


def trig(rows, cols, length):
    angle = (rows[:, None] * cols[None, :] % length) * (2.0 * math.pi / length)
    scale = 1.0 / math.sqrt(length)
    return np.cos(angle) * scale, np.sin(angle) * scale


def as_bf16(table):
    return jnp.asarray(table.astype(np.float32)).astype(BF)


def left_tables(length):
    half = np.arange(length // 2)
    tables = []
    for parity in (0, 1):
        c, s = trig(half, 2 * half + parity, length)
        tables.append(np.block([[c, -s], [s, c]]))
    return as_bf16(np.stack(tables))


def right_inverse(length):
    full = np.arange(length)
    c, s = trig(full, full, length)
    return as_bf16(np.block([[c, s], [-s, c]]))


def projector_tables(length):
    half = np.arange(length // 2)
    first, second = [], []
    for parity in (0, 1):
        c, s = trig(half, 2 * half + parity, length)
        first.append(np.block([[c, -s], [s, c]]))
        second.append(np.block([[c.T, s.T], [-s.T, c.T]]))
    return as_bf16(np.stack(first)), as_bf16(np.stack(second))


def cost(micros):
    return pl.CostEstimate(flops=int(micros * 1.0e9), bytes_accessed=0, transcendentals=0)


def dot(a, b):
    return jnp.dot(a, b, preferred_element_type=F32)


def in_hbm(value):
    return pltpu.with_memory_space_constraint(value, pltpu.HBM)


def joined(real, imag):
    return jnp.concatenate([real.astype(BF), imag.astype(BF)], 1)


def data_kernel(group, ids, *refs):
    count = group * LANE_BLOCKS
    refs = refs[: count + 5 + group] + refs[-2:]
    maps, left, right, first, second = refs[count : count + 5]
    masks = refs[count + 5 : count + 5 + group]
    out, proj = refs[count + 5 + group :]
    coils, rows, wide = maps.shape
    width, half = wide // 2, rows // 2
    for g in range(group):
        kd = refs[g * LANE_BLOCKS : (g + 1) * LANE_BLOCKS]
        mask = masks[g][0].astype(BF)
        keep = mask[:, :wide]
        masked = []
        for c in range(coils):
            parts = []
            for e in range(2):
                lines = [part[0, c, pl.ds(e, half, stride=2), :].astype(BF) for part in kd]
                real, imag = lines[: LANE_BLOCKS // 2], lines[LANE_BLOCKS // 2 :]
                stacked = jnp.concatenate([jnp.concatenate(real, 1), jnp.concatenate(imag, 1)], 0)
                parts.append(dot(left[e], stacked))
            uppers, lowers = [], []
            for r in range(0, half, TILE):
                at, to = slice(r, r + TILE), slice(half + r, half + r + TILE)
                uppers.append(joined(parts[0][at] + parts[1][at], parts[0][to] + parts[1][to]) * keep)
                lowers.append(joined(parts[0][at] - parts[1][at], parts[0][to] - parts[1][to]) * keep)
            masked += uppers + lowers
        back = dot(jnp.concatenate(masked, 0), right[...])
        for e in range(2):
            lhs = first[e] * mask[:, wide + e * width : wide + (e + 1) * width]
            proj[g, e] = dot(lhs, second[e]).astype(BF)
        for r in range(0, rows, TILE):
            real, imag = None, None
            for c in range(coils):
                line = back[c * rows + r : c * rows + r + TILE]
                br, bi = line[:, :width], line[:, width:]
                sr, si = maps[c, r : r + TILE, :width], maps[c, r : r + TILE, width:]
                tr, ti = sr * br + si * bi, sr * bi - si * br
                real, imag = (tr, ti) if real is None else (real + tr, imag + ti)
            out[g, r : r + TILE] = joined(real, imag)


def data_term(ids, kdata, maps, masks, tables, after, spill, group=2):
    phases, coils, rows, wide = kdata.shape
    count = ids.shape[0]
    lanes = wide // LANE_BLOCKS
    whole = lambda a: pl.BlockSpec(a.shape, lambda i, ids: (0,) * a.ndim)
    lines = lambda g, q: pl.BlockSpec(
        (1, coils, rows, lanes), lambda i, ids: (ids[group * i + g], 0, 0, q)
    )
    row = lambda g: pl.BlockSpec(
        (1,) + masks.shape[1:], lambda i, ids: (ids[group * i + g], 0, 0)
    )
    return pl.pallas_call(
        functools.partial(data_kernel, group),
        grid_spec=pltpu.PrefetchScalarGridSpec(
            num_scalar_prefetch=1,
            grid=(count // group,),
            in_specs=[lines(g, q) for g in range(group) for q in range(LANE_BLOCKS)]
            + [whole(a) for a in (maps,) + tables]
            + [row(g) for g in range(group)]
            + [pl.BlockSpec(memory_space=pl.ANY)] * len(after),
            out_specs=[
                pl.BlockSpec((group, rows, wide), lambda i, ids: (i, 0, 0)),
                pl.BlockSpec((group, 2, wide // 2, wide // 2), lambda i, ids: (i, 0, 0, 0)),
            ],
        ),
        out_shape=[
            (pltpu.HBM if spill else jax.ShapeDtypeStruct)((count, rows, wide), BF),
            (pltpu.HBM if spill else jax.ShapeDtypeStruct)((count, 2, wide // 2, wide // 2), BF),
        ],
        compiler_params=pltpu.CompilerParams(vmem_limit_bytes=24 * MIB),
        cost_estimate=cost(1.1 * count),
        name="data_term",
    )(ids, *[in_hbm(kdata)] * (group * LANE_BLOCKS), maps, *tables, *[masks] * group, *after)


def image_kernel(ids, place, far_a, far_b, near_a, near_b, maps, data, proj, noise_a, noise_b, *rest):
    away, mine, held = rest[-3:]
    step = pl.program_id(0)
    coils, rows, wide = maps.shape
    width, quarter = wide // 2, wide // 4
    strip = noise_a.shape[1]

    @pl.when(step == 0)
    def _():
        held[0] = far_a[0]
        held[1] = far_b[0]

    @pl.when(step == 1)
    def _():
        held[0] = near_a[0]
        held[1] = near_b[0]

    at = pl.ds(pl.multiple_of(place[0], strip), strip)
    for g, noise in enumerate((noise_a, noise_b)):
        plus, minus = [], []
        for c in range(coils):
            for r in range(0, rows, TILE):
                to = slice(r, r + TILE)
                xr, xi = held[g, to, :width].astype(F32), held[g, to, width:].astype(F32)
                sr, si = maps[c, to, :width], maps[c, to, width:]
                cr, ci = sr * xr - si * xi, sr * xi + si * xr
                cr0, cr1, ci0, ci1 = cr[:, :quarter], cr[:, quarter:], ci[:, :quarter], ci[:, quarter:]
                plus.append(joined(cr0 + cr1, ci0 + ci1))
                minus.append(joined(cr0 - cr1, ci0 - ci1))
        even = dot(jnp.concatenate(plus, 0), proj[g, 0])
        odd = dot(jnp.concatenate(minus, 0), proj[g, 1])
        for r in range(0, rows, TILE):
            to = slice(r, r + TILE)
            real = -data[g, to, :width].astype(F32)
            imag = -data[g, to, width:].astype(F32)
            for c in range(coils):
                sr, si = maps[c, to, :width], maps[c, to, width:]
                p, q = even[c * rows + r : c * rows + r + TILE], odd[c * rows + r : c * rows + r + TILE]
                low, high = p + q, p - q
                br = jnp.concatenate([low[:, :quarter], high[:, :quarter]], 1)
                bi = jnp.concatenate([low[:, quarter:], high[:, quarter:]], 1)
                real = real + sr * br + si * bi
                imag = imag + sr * bi - si * br
            held[g, to, :] = joined(real, imag)
        held[g, at, :] = (held[g, at, :].astype(F32) + WEIGHT_RED * noise[0]).astype(BF)

    @pl.when(step == 0)
    def _():
        away[...] = held[...]

    @pl.when(step == 1)
    def _():
        mine[...] = held[...]


def image_term(ids, place, images, maps, data, proj, noise, chunk, after):
    coils, rows, wide = maps.shape
    strip, width = noise.shape[1], wide // 2
    whole = lambda a: pl.BlockSpec(a.shape, lambda i, ids, place: (0,) * a.ndim)
    extra = lambda g: pl.BlockSpec((1, strip, wide), lambda i, ids, place: (ids[2 * i + g], 0, 0))
    return pl.pallas_call(
        image_kernel,
        grid_spec=pltpu.PrefetchScalarGridSpec(
            num_scalar_prefetch=2,
            grid=(2,),
            in_specs=[
                *[whole(a) for a in images],
                whole(maps),
                pl.BlockSpec((2, rows, wide), lambda i, ids, place: (2 * chunk + i, 0, 0)),
                pl.BlockSpec((2, 2, width, width), lambda i, ids, place: (2 * chunk + i, 0, 0, 0)),
                extra(0),
                extra(1),
            ]
            + [pl.BlockSpec(memory_space=pl.ANY)] * len(after),
            out_specs=[pl.BlockSpec((2, rows, wide), lambda i, ids, place: (0, 0, 0))] * 2,
            scratch_shapes=[pltpu.VMEM((2, rows, wide), BF)],
        ),
        out_shape=[jax.ShapeDtypeStruct((2, rows, wide), BF)] * 2,
        compiler_params=pltpu.CompilerParams(vmem_limit_bytes=16 * MIB),
        cost_estimate=cost(5.0),
        name="image_term",
    )(ids, place, *images, maps, data, proj, noise, noise, *after)


def shifted(value, step):
    if step == 1:
        return value
    width = value.shape[1]
    lane = lax.broadcasted_iota(jnp.int32, value.shape, 1)
    if step == 0:
        return jnp.where(lane == 0, 0.0, pltpu.roll(value, 1, 1))
    return jnp.where(lane == width - 1, 0.0, pltpu.roll(value, width - 1, 1))


def conv_kernel(ch, place, strips, w1, w2, w3, pick1, pick2, spread3, *rest):
    out, x1, h1, noise, a1, a2, a3 = rest[-7:]
    phases, tall, wide = strips.shape
    width = wide // 2
    strip = tall - 8
    n1, n2, n3 = strip + 4, (strip + 2) // 2, strip + 2
    image_rows = strip * phases
    top = jnp.where(place[0] == 0, 0.0, 1.0)
    bottom = jnp.where(place[0] + strip == image_rows, 0.0, 1.0)

    base = None
    for tap in range(27):
        part = lax.dot_general(w1[tap], pick1[tap], (((0,), (0,)), ((), ())), preferred_element_type=F32)
        base = part if base is None else base + part
    for j in range(n1):
        line = base if j == 0 else pltpu.roll(base, j, 1)
        a1[j * ch : (j + 1) * ch] = line[:, : a1.shape[1]].astype(BF)
    tiles = [jnp.zeros((ch, 128), F32)] * (-(-a2.shape[1] // 128))
    for tap in range(27):
        d, e, f = tap // 9, tap // 3 % 3, tap % 3
        at = ((d * 3 + f) * (n2 + 2) + e) * ch
        tiles[at // 128] = tiles[at // 128] + dot(w2[tap], pick2[at % 128 // ch])
    base = jnp.concatenate(tiles, 1)
    for j in range(n2):
        line = base if j == 0 else pltpu.roll(base, j * ch, 1)
        a2[j * ch : (j + 1) * ch] = line[:, : a2.shape[1]].astype(BF)
    lines = [dot(w3[tap], spread3[...]) for tap in range(27)]
    row = lax.broadcasted_iota(jnp.int32, (strip, spread3.shape[1]), 0)
    lane = lax.broadcasted_iota(jnp.int32, (strip, spread3.shape[1]), 1)
    for k in range(18):
        line = None
        for e in range(3):
            inside = (lane >= (row + e) * ch) & (lane < (row + e + 1) * ch)
            d, f, o = k // 6, k // 2 % 3, k % 2
            part = jnp.where(inside, lines[(d * 3 + e) * 3 + f][o : o + 1], 0.0)
            line = part if line is None else line + part
        a3[k * strip : (k + 1) * strip] = line[:, : a3.shape[1]].astype(BF)

    def inside_rows(value, rows):
        edge = rows * ch
        middle = value[edge : value.shape[0] - edge]
        return jnp.concatenate([value[:edge] * top, middle, value[value.shape[0] - edge :] * bottom], 0)

    def load(p, carry):
        image = strips[p].astype(F32)
        both = jnp.concatenate([image[:, :width], image[:, width:]], 0)
        for f in range(3):
            x1[p + 1, f * 2 * tall : (f + 1) * 2 * tall] = shifted(both, f).astype(BF)
        return carry

    lax.fori_loop(0, phases, load, 0, unroll=4)
    x1[0] = x1[phases]
    x1[phases + 1] = x1[1]

    def first(p, carry):
        stacked = x1[pl.ds(p, 3)].reshape(18 * tall, width)
        value = inside_rows(jnp.maximum(dot(a1[...], stacked), 0.0), 2)
        for f in range(3):
            h1[p + 1, f] = shifted(value, f).astype(BF)
        return carry

    lax.fori_loop(0, phases, first, 0, unroll=16)
    h1[0] = h1[phases]
    h1[phases + 1] = h1[1]
    noise[...] = jnp.zeros_like(noise)

    def second(p, carry):
        blocks = []
        for b in range(2):
            lo = b * n2 * ch
            stacked = h1[pl.ds(p, 3), :, lo : lo + (n2 + 2) * ch, :]
            stacked = stacked.reshape(9 * (n2 + 2) * ch, width)
            blocks.append(dot(a2[...], stacked))
        value = inside_rows(jnp.maximum(jnp.concatenate(blocks, 0), 0.0), 1)
        spread = dot(a3[...], value.astype(BF))
        for d in range(3):
            part = None
            for f in range(3):
                lo = (d * 3 + f) * 2 * strip
                piece = shifted(spread[lo : lo + 2 * strip], f)
                part = piece if part is None else part + piece
            noise[p + 2 - d] += part
        return carry

    lax.fori_loop(0, phases, second, 0, unroll=16)
    noise[phases] += noise[0]
    noise[1] += noise[phases + 1]

    def store(p, carry):
        both = noise[p + 1]
        out[p, :, :width] = both[:strip]
        out[p, :, width:] = both[strip:]
        return carry

    lax.fori_loop(0, phases, store, 0, unroll=4)


def pick_tables(cin, tall, ch, n3):
    pad = lambda n: -(-n // 128) * 128
    pick1 = np.zeros((27, cin, pad(9 * cin * tall)), np.float32)
    for d in range(3):
        for e in range(3):
            for f in range(3):
                for c in range(cin):
                    pick1[(d * 3 + e) * 3 + f, c, ((d * 3 + f) * cin + c) * tall + 1 + e] = 1.0
    pick2 = np.zeros((128 // ch, ch, 128), np.float32)
    for slot in range(128 // ch):
        pick2[slot, :, slot * ch : (slot + 1) * ch] = np.eye(ch)
    spread3 = np.zeros((ch, pad(n3 * ch)), np.float32)
    for c in range(ch):
        spread3[c, c : n3 * ch : ch] = 1.0
    return as_bf16(pick1), as_bf16(pick2), as_bf16(spread3)


def denoise(strips, w_first, w_middle, w_last, place, after):
    phases, tall, wide = strips.shape
    strip, width, (ch, cin) = tall - 8, wide // 2, w_first.shape[:2]
    n1, n2, n3 = strip + 4, (strip + 2) // 2, strip + 2
    picks = pick_tables(cin, tall, ch, n3)
    weights = (
        jnp.transpose(w_first, (2, 3, 4, 1, 0)).reshape(27, cin, ch),
        jnp.transpose(w_middle, (2, 3, 4, 0, 1)).reshape(27, ch, ch),
        jnp.transpose(w_last, (2, 3, 4, 0, 1)).reshape(27, 2, ch),
    )
    vmem = pl.BlockSpec(memory_space=pltpu.VMEM)
    return pl.pallas_call(
        functools.partial(conv_kernel, ch),
        in_specs=[pl.BlockSpec(memory_space=pltpu.SMEM)]
        + [vmem] * 7
        + [pl.BlockSpec(memory_space=pl.ANY)] * len(after),
        out_specs=vmem,
        out_shape=jax.ShapeDtypeStruct((phases, strip, wide), F32),
        scratch_shapes=[
            pltpu.VMEM((phases + 2, 6 * tall, width), BF),
            pltpu.VMEM((phases + 2, 3, n1 * ch, width), BF),
            pltpu.VMEM((phases + 2, 2 * strip, width), F32),
            pltpu.VMEM((n1 * ch, 9 * cin * tall), BF),
            pltpu.VMEM((n2 * ch, 9 * (n2 + 2) * ch), BF),
            pltpu.VMEM((18 * strip, n3 * ch), BF),
        ],
        compiler_params=pltpu.CompilerParams(vmem_limit_bytes=20 * MIB),
        cost_estimate=cost(13.0),
        name="denoise",
    )(place, strips, *[in_hbm(a) for a in weights + picks], *after)


def prepare_kernel(estimate, mask, pick, image, strips, masks, padded):
    rows, wide = estimate.shape[1:]
    phases, tall = strips.shape[:2]
    strip = tall - 8
    value = estimate[0]
    image[0] = value.astype(BF)
    edge = jnp.zeros((4, wide), F32)
    padded[0:4] = edge
    padded[rows + 4 : rows + 8] = edge
    padded[4 : rows + 4] = value
    for j in range(phases):
        strips[j] = padded[j * strip : j * strip + tall].astype(BF)
    spread = dot(mask[...].astype(F32).astype(BF), pick[...])
    for p in range(phases):
        masks[p] = spread[p : p + 1]


def prepare(estimate, mask):
    rows, wide = estimate.shape[1:]
    phases, width = mask.shape
    tall = rows // phases + 8
    pick = np.zeros((width, 4 * width), np.float32)
    half = width // 2
    for k in range(width):
        pick[k, [k, width + k]] = 1.0
        at = 2 * width + (k % 2) * width + k // 2
        pick[k, [at, at + half]] = 1.0
    return pl.pallas_call(
        prepare_kernel,
        out_shape=[
            jax.ShapeDtypeStruct((1, rows, wide), BF),
            jax.ShapeDtypeStruct((phases, tall, wide), BF),
            jax.ShapeDtypeStruct((phases, 1, 4 * width), F32),
        ],
        scratch_shapes=[pltpu.VMEM((rows + 8, wide), F32)],
        cost_estimate=cost(2.0),
        name="prepare",
    )(estimate, mask, as_bf16(pick))


def shards(estimate, kdata, maps, mask, w_first, w_middle, w_last):
    count = lax.axis_size("phase")
    me = lax.axis_index("phase")
    planes = count // 4
    rows, wide = estimate.shape[1:]
    strip = rows // count
    tables = (left_tables(rows), right_inverse(wide // 2)) + projector_tables(wide // 2)
    place = (me * strip).astype(jnp.int32)[None]

    def send(value, shift=0, flip=0):
        pairs = [(i, ((i ^ flip) + 4 * shift) % count) for i in range(count)]
        return lax.ppermute(value, "phase", pairs)

    def behind(value, *earlier):
        return lax.optimization_barrier((value,) + earlier)[0]

    order = list(dict.fromkeys([planes // 2, 0] + list(range(planes))))
    lead, rest = order[:2], order[2:]
    flips = jnp.array([1, 3, 0, 2], jnp.int32)
    ids = {k: ((me ^ flips) + 4 * k) % count for k in order}

    image, strips, masks = prepare(estimate, mask)
    own, across, images, terms = {0: image}, {}, {}, {}
    far = order[0]
    if far:
        own[far] = send(image, shift=planes - far)
    across[0] = send(image, flip=2)
    strips = lax.all_to_all(strips, "phase", 0, 0, tiled=True)

    def data_of(chunks, after):
        both = jnp.concatenate([ids[k] for k in chunks])
        data, proj = data_term(both, kdata, maps, masks, tables, after, chunks is lead)
        for n, k in enumerate(chunks):
            terms[k] = (data, proj, n)
        return data

    def gather(k):
        images[k] = (send(own[k], flip=1), send(across[k], flip=1), own[k], across[k])

    pairs, planed = {}, {}

    def start(k, after):
        data, proj, n = terms[k]
        away, mine = image_term(ids[k], place, images[k], maps, data, proj, noise, n, after)
        pairs[k] = mine.astype(F32) + send(away, flip=1).astype(F32)

    def finish(k, earlier=()):
        other = behind(pairs[k][1].astype(BF), *earlier)
        plane = (pairs[k][0] + send(other, flip=2).astype(F32)).astype(BF)
        planed[k] = (plane, send(plane, shift=k) if k else plane)

    first = data_of(lead, ())
    gather(0)
    for k in rest:
        own[k] = send(behind(image, own[far]), shift=planes - k)
    if far:
        across[far] = send(own[far], flip=2)
    noise = denoise(strips, w_first, w_middle, w_last, place, (first, own[far], across[0]))
    if far:
        across[far] = behind(across[far], noise)
        gather(far)
    for k in rest:
        across[k] = send(own[k], flip=2)

    for k in lead:
        start(k, tuple(own[r] for r in rest))
        finish(k)
    for k in rest:
        gather(k)
    if rest:
        data_of(rest, tuple(pairs[k] for k in lead) + (noise, across[rest[0]]))
    for n, k in enumerate(rest):
        if n == 0:
            start(k, (planed[order[0]][0],) + tuple(across[r] for r in rest[1:]))
        else:
            start(k, (pairs[rest[n - 1]],))
        finish(k, (planed[order[n - 1]][1],) if n else ())
    total = sum(planed[k][1].astype(F32) for k in order)
    return estimate - STEP_SIZE * total[None]


def solution(mesh):
    return jax.shard_map(
        shards,
        mesh=mesh,
        in_specs=(
            P(("slab", "phase"), None, None),
            P("slab", "phase", None, None),
            P(("slab", "phase"), None, None),
            P("slab", None),
            P(),
            P(),
            P(),
        ),
        out_specs=P(("slab", "phase"), None, None),
        check_vma=False,
    )
```
